32 devices in a mesh: groups: 2 (over y), fsdp: 16 (over z, x, core).
Axes of the slice: x: 2, y: 2, z: 4, core: 2. Of those that a mesh axis runs over, the one named last changes fastest.
Arguments:
- tokens: bfloat16 [4096, 8192], P(('groups', 'fsdp')), parts along dimension 0, may hold values from -6 to 6
- grad_out: bfloat16 [4096, 1024], P(('groups', 'fsdp')), parts along dimension 0, may hold values from -6 to 6
- base_weight: bfloat16 [8192, 1024], P('fsdp'), may hold values from -0.0625 to 0.0625
- shrink_factor: bfloat16 [128, 8192, 128], P('groups', 'fsdp'), parts along dimension 0, may hold values from -0.0625 to 0.0625
- expand_factor: bfloat16 [128, 128, 1024], P('groups', 'fsdp'), parts along dimension 0, may hold values from -0.5 to 0.5
- rank_per_adapter: int32 [128], P('groups'), parts along dimension 0, may hold values from 16 to 128, as said below
- block_adapter: int32 [32], P('groups'), parts along dimension 0, may hold values from 0 to 63
- block_rows: int32 [32], P(('groups', 'fsdp')), parts along dimension 0, may hold values from 32 to 128, as said below
Outputs:
- projected: bfloat16 [4096, 1024], P(('groups', 'fsdp')), parts along dimension 0
- token_input_gradient: bfloat16 [4096, 8192], P(('groups', 'fsdp')), parts along dimension 0
- shrink_grad: float32 [128, 8192, 128], P('groups', 'fsdp'), parts along dimension 0
- expand_grad: float32 [128, 128, 1024], P('groups', 'fsdp'), parts along dimension 0
The draws below stay inside these ranges and needn't reach their ends.
There are 2 independent parts, one for each index of `groups`. The reference program is written for one: setup_inputs(seed, part) draws one part's arguments, and reference() takes and returns one part's arrays. A program takes and returns all parts, laid end to end along the dimension named above; an argument that names none is the same for every part. Nothing has to cross between parts.
Inputs may be any that keep to these rules, and one draw needn't show every extreme that they name: `rank_per_adapter`: every rank is a power of two; some adapter has rank 128 and some has rank 16. `block_rows`: some block has all 128 rows valid and some has 32.
All inputs are finite; a program needn't handle non-finite values.
Results may differ from the reference program's by a relative error of at most 0.0044.
Values may be sent and summed in bfloat16 or wider, within the bound.
No kernel may reach another device: no remote copies, remote signals or barrier semaphores. Data moves between devices by JAX's collectives and lax.ppermute only.
A program may use at most 128 MiB of HBM per device.

```python
import math
import jax
import jax.numpy as jnp
import numpy as np
from jax import lax

D = 8192
KV = 1024
R = 128
ADAPTERS = 64
BLOCK = 128
TOKENS = 2048
TOKEN_BLOCKS = 16


def draw_rank_per_adapter(key, part):
    key = jax.random.fold_in(key, 11)
    key_power, key_top, key_low = jax.random.split(key, 3)
    exponent = jax.random.randint(key_power, (ADAPTERS,), 4, R.bit_length()).astype(jnp.int32)
    rank_list = jnp.left_shift(jnp.ones((ADAPTERS,), jnp.int32), exponent)
    top_at = jax.random.randint(key_top, (), 0, ADAPTERS)
    low_at = (top_at + jax.random.randint(key_low, (), 1, ADAPTERS)) % ADAPTERS
    rank_list = rank_list.at[top_at].set(R).at[low_at].set(16)
    return rank_list.astype(jnp.int32)


def draw_block_rows(key, part):
    key = jax.random.fold_in(key, 23)
    key_rows, key_top, key_low = jax.random.split(key, 3)
    row_list = jax.random.randint(key_rows, (TOKEN_BLOCKS,), BLOCK // 4, BLOCK + 1)
    top_at = jax.random.randint(key_top, (), 0, TOKEN_BLOCKS)
    low_at = (top_at + jax.random.randint(key_low, (), 1, TOKEN_BLOCKS)) % TOKEN_BLOCKS
    row_list = row_list.at[top_at].set(BLOCK).at[low_at].set(BLOCK // 4)
    return row_list.astype(jnp.int32)


def set_ends(entries, rng, smallest, top_value):
    index_at = [jax.random.randint(jax.random.fold_in(rng, axis), (), 0, length) for axis, length in enumerate(entries.shape)]
    main_axis = entries.shape.index(max(entries.shape))
    next_to = index_at[:main_axis] + [(index_at[main_axis] + 1) % entries.shape[main_axis]] + index_at[main_axis + 1:]
    return entries.at[tuple(index_at)].set(smallest).at[tuple(next_to)].set(top_value)


def block_scale(stream_key, extent, shards, smallest, high):
    level, own = 1.0, jax.random.fold_in(stream_key, 6)
    for position, blocks in shards:
        steps = jnp.exp(jax.random.uniform(jax.random.fold_in(own, position), (blocks,), jnp.float32, smallest / len(shards), high / len(shards)))
        level = level * jnp.repeat(steps, extent[position] // blocks).reshape([-1 if axis == position else 1 for axis in range(len(extent))])
    return level


def rank_table(number_of, slope):
    loads = [(1 << 20) // math.isqrt(rank ** slope) + 1 for rank in range(1, number_of + 1)]
    width = 1 + sum(loads) // (1 << 30)
    return np.cumsum(np.array([max(1, weight // width) for weight in loads]))


def ranked_ids(rng, dims, number_of, skew):
    table = rank_table(number_of, skew)
    pick = jax.random.randint(jax.random.fold_in(rng, 1), dims, 0, int(table[number_of - 1]))
    standing = jnp.searchsorted(jnp.asarray(table, jnp.int32), pick, side="right")
    return jax.random.permutation(jax.random.fold_in(rng, 2), number_of)[standing].astype(jnp.int32)


def scatter_about(own_key, shape, deviation, most, shards=(), kind=jnp.bfloat16):
    drawn = jax.random.normal(own_key, shape, jnp.float32) * deviation
    if len(shards) > 0:
        drawn = block_scale(own_key, shape, shards, -0.22, 0.18) * drawn
    return jnp.clip(drawn, min=-most, max=most).astype(kind)


def setup_inputs(seed: int = 0, part: int = 0) -> dict:
    arg_keys = jax.random.split(jax.random.key(seed), 9)
    own_keys = jax.random.split(jax.random.fold_in(arg_keys[8], part), 9)
    return {
        "tokens": scatter_about(own_keys[0], (TOKENS, D), 1.0, 6.0, ((0, 16),)),
        "grad_out": scatter_about(own_keys[1], (TOKENS, KV), 1.0, 6.0, ((0, 16),)),
        "base_weight": scatter_about(arg_keys[2], (D, KV), D ** -0.5, 0.0625, ((0, 16),)),
        "shrink_factor": scatter_about(own_keys[3], (ADAPTERS, D, R), D ** -0.5, 0.0625, ((1, 16),)),
        "expand_factor": scatter_about(own_keys[4], (ADAPTERS, R, KV), R ** -0.5, 0.5, ((1, 16),)),
        "rank_per_adapter": draw_rank_per_adapter(jax.random.fold_in(jax.random.fold_in(arg_keys[8], part), 71), part),
        "block_adapter": set_ends(ranked_ids(own_keys[6], (TOKEN_BLOCKS,), ADAPTERS, 2), jax.random.fold_in(own_keys[6], 3), 0, ADAPTERS - 1).astype(jnp.int32),
        "block_rows": draw_block_rows(jax.random.fold_in(jax.random.fold_in(arg_keys[8], part), 71), part),
    }


ADAPTER_STRENGTH = 16.0

def block_terms(x_block, e_block, in_factor, out_factor, scaling, rank_now, columns, rank_cap):
    in_part = in_factor[:, :columns]
    out_part = out_factor[:columns, :]
    kept_cols = lax.iota(jnp.int32, columns)[None, :] < rank_now
    shrink = jnp.dot(x_block, in_part, preferred_element_type=jnp.float32)
    shrink = jnp.where(kept_cols, shrink, 0.0).astype(jnp.bfloat16)
    expand_matrix = jnp.dot(shrink, out_part, preferred_element_type=jnp.float32) * scaling
    back_grad = lax.dot_general(e_block, out_part, (((1,), (1,)), ((), ())), preferred_element_type=jnp.float32) * scaling
    back_grad = jnp.where(kept_cols, back_grad, 0.0).astype(jnp.bfloat16)
    input_portion = lax.dot_general(back_grad, in_part, (((1,), (1,)), ((), ())), preferred_element_type=jnp.float32)
    gradient_down = lax.dot_general(x_block, back_grad, (((0,), (0,)), ((), ())), preferred_element_type=jnp.float32)
    grad_out_f = lax.dot_general(shrink, e_block, (((0,), (0,)), ((), ())), preferred_element_type=jnp.float32) * scaling
    padding = rank_cap - columns
    back_grad = jnp.pad(back_grad, ((0, 0), (0, padding)))
    gradient_down = jnp.pad(gradient_down, ((0, 0), (0, padding)))
    grad_out_f = jnp.pad(grad_out_f, ((0, padding), (0, 0)))
    return (expand_matrix, input_portion, back_grad, gradient_down, grad_out_f)

def reference(tokens, grad_out, base_weight, shrink_factor, expand_factor, rank_per_adapter, block_adapter, block_rows):
    row_valid = (lax.iota(jnp.int32, BLOCK)[None, :] < block_rows[:, None]).reshape(TOKENS, 1)
    masked = jnp.where(row_valid, grad_out, jnp.zeros((), grad_out.dtype))
    frozen_output = jnp.dot(tokens, base_weight, preferred_element_type=jnp.float32)
    frozen_backward = lax.dot_general(masked, base_weight, (((1,), (1,)), ((), ())), preferred_element_type=jnp.float32)
    adapter_scales = ADAPTER_STRENGTH / jnp.sqrt(rank_per_adapter.astype(jnp.float32))

    def accumulate_sums(index, running_sums):
        adapter_output, adapter_input, gradient_down, gradient_upward = running_sums
        block_idx = jnp.asarray(index).astype(jnp.int32)
        starting_row = block_idx * BLOCK
        x_block = lax.dynamic_slice_in_dim(tokens, starting_row, BLOCK, 0)
        e_block = lax.dynamic_slice_in_dim(masked, starting_row, BLOCK, 0)
        adapter = lax.dynamic_index_in_dim(block_adapter, block_idx, 0, keepdims=False).astype(jnp.int32)
        in_factor = lax.dynamic_index_in_dim(shrink_factor, adapter, 0, keepdims=False)
        out_factor = lax.dynamic_index_in_dim(expand_factor, adapter, 0, keepdims=False)
        scaling = lax.dynamic_index_in_dim(adapter_scales, adapter, 0, keepdims=False)
        rank_now = lax.dynamic_index_in_dim(rank_per_adapter, adapter, 0, keepdims=False)
        expand_matrix, input_portion, back_grad, part_in, part_up = block_terms(x_block, e_block, in_factor, out_factor, scaling, rank_now, R, R)
        adapter_output = lax.dynamic_update_slice_in_dim(adapter_output, expand_matrix, starting_row, 0)
        adapter_input = lax.dynamic_update_slice_in_dim(adapter_input, input_portion, starting_row, 0)
        old_in = lax.dynamic_index_in_dim(gradient_down, adapter, 0, keepdims=False)
        gradient_down = lax.dynamic_update_index_in_dim(gradient_down, old_in + part_in, adapter, 0)
        old_up = lax.dynamic_index_in_dim(gradient_upward, adapter, 0, keepdims=False)
        gradient_upward = lax.dynamic_update_index_in_dim(gradient_upward, old_up + part_up, adapter, 0)
        return (adapter_output, adapter_input, gradient_down, gradient_upward)
    initial_running_sums = (jnp.zeros((TOKENS, KV), jnp.float32), jnp.zeros((TOKENS, D), jnp.float32), jnp.zeros((ADAPTERS, D, R), jnp.float32), jnp.zeros((ADAPTERS, R, KV), jnp.float32))
    adapter_output, adapter_input, gradient_down, gradient_upward = lax.fori_loop(0, TOKEN_BLOCKS, accumulate_sums, initial_running_sums)
    projected = (frozen_output + adapter_output).astype(jnp.bfloat16)
    token_input_gradient = (frozen_backward + adapter_input).astype(jnp.bfloat16)
    return (projected, token_input_gradient, gradient_down, gradient_upward)
```

```python
import jax
import jax.numpy as jnp
from jax import lax
from jax.experimental import pallas as pl
from jax.experimental.pallas import tpu as pltpu
from jax.sharding import PartitionSpec as P

BLOCK = 128
ADAPTER_STRENGTH = 16.0
INNER = 4
MIB = 1 << 20
BF = jnp.bfloat16
F32 = jnp.float32

HBM = pl.BlockSpec(memory_space=pltpu.HBM)
VM = pl.BlockSpec(memory_space=pltpu.VMEM)
SM = pl.BlockSpec(memory_space=pltpu.SMEM)


def params(mib):
    return pltpu.CompilerParams(vmem_limit_bytes=mib * MIB)


COST = pl.CostEstimate(flops=1, bytes_accessed=1, transcendentals=0)


def dot(a, b, ca, cb):
    return lax.dot_general(a, b, (((ca,), (cb,)), ((), ())), preferred_element_type=F32)


def adapter_scale(rank):
    return ADAPTER_STRENGTH / jnp.sqrt(jnp.full((BLOCK, BLOCK), rank, jnp.int32).astype(F32))


def pick_kernel(outer, me_ref, ids_ref, factor, s_send, s_keep, sem):
    def start(i, carry):
        core = lax.div(i, outer)
        own = jnp.bitwise_xor(me_ref[0], lax.rem(i, outer) * INNER + core)
        pltpu.make_async_copy(factor.at[ids_ref[own]], s_keep.at[i], sem.at[0]).start()
        far = jnp.bitwise_xor(own, 2)
        pltpu.make_async_copy(factor.at[ids_ref[far]], s_send.at[i], sem.at[1]).start()
        return carry

    half = s_keep.shape[0]
    lax.fori_loop(0, half, start, 0)
    pltpu.make_async_copy(factor.at[pl.ds(0, half)], s_keep, sem.at[0]).wait()
    pltpu.make_async_copy(factor.at[pl.ds(0, half)], s_send, sem.at[1]).wait()


def pick(me, ids, factor, outer):
    picked = jax.ShapeDtypeStruct((2 * outer,) + factor.shape[1:], BF)
    return pl.pallas_call(
        lambda *refs: pick_kernel(outer, *refs),
        out_shape=(picked, picked),
        in_specs=[SM, SM, HBM],
        out_specs=(VM, VM),
        scratch_shapes=[pltpu.SemaphoreType.DMA((2,))],
        compiler_params=params(57),
        cost_estimate=COST,
        name="pick_factors",
    )(me, ids, factor)


def first_kernel(outer, me_ref, ids_ref, ranks_ref, rows_ref, tokens, grad, up_ref, *outs):
    rank = ranks_ref[ids_ref[me_ref[0]]]
    plane = lax.div(me_ref[0], INNER)
    dz = tokens.shape[1] // outer
    kv = grad.shape[1]
    rows = lax.broadcasted_iota(jnp.int32, grad.shape, 0)
    masked = jnp.where(rows < rows_ref[0], grad[...].astype(F32), 0.0).astype(BF)
    back = dot(masked, up_ref[...], 1, 1) * adapter_scale(rank)
    cols = lax.broadcasted_iota(jnp.int32, back.shape, 1)
    back = jnp.where(cols < rank, back, 0.0).astype(BF)
    for k, out in enumerate(outs):
        at = pl.multiple_of(jnp.bitwise_xor(plane, k) * dz, dz)
        out[:, :dz] = tokens[:, pl.ds(at, dz)]
        out[:, dz : dz + kv] = masked
        out[:, dz + kv :] = back


def first_sends(me, ids, ranks, block_rows, tokens, grad, up, outer):
    rows, width = tokens.shape
    wide = width // outer + grad.shape[1] + up.shape[0]
    return pl.pallas_call(
        lambda *refs: first_kernel(outer, *refs),
        out_shape=tuple(jax.ShapeDtypeStruct((rows, wide), BF) for _ in range(outer)),
        in_specs=[SM] * 4 + [VM] * 3,
        out_specs=(VM,) * outer,
        compiler_params=params(24),
        cost_estimate=COST,
        name="first_sends",
    )(me, ids, ranks, block_rows, tokens, grad, up)


def plane_parts(me, w, s, scratch, outer, sub):
    own = lax.rem(me, INNER)
    parts = []
    for j, (ws, (ref, at)) in enumerate(zip(w, s)):
        first = pl.multiple_of(jnp.bitwise_xor(own, j) * sub, sub)
        row = 0
        for weight in ws:
            size = weight.shape[0]
            rows = slice(row, row + size)
            if scratch:
                wz, sz = scratch
                base = pl.multiple_of(first + row, size)
                wz[pl.ds(base, size), :] = weight[...]
                for k in range(outer):
                    sz[k, pl.ds(base, size), :] = ref[at + k, rows, :]
            else:
                base = pl.multiple_of(first + row, size)
                factors = [ref.at[at + k, rows] for k in range(outer)]
                parts.append((base, size, weight, factors))
            row += size
    if scratch:
        wz, sz = scratch
        parts = [(0, wz.shape[0], wz, [sz.at[k] for k in range(outer)])]
    return parts


def plane_scratch(outer, sub, kv, rank):
    if sub % 256 == 0:
        return []
    dz = sub * INNER
    return [pltpu.VMEM((dz, kv), BF), pltpu.VMEM((outer, dz, rank), BF)]


def main_kernel(outer, sub, kv, me_ref, *refs):
    w = [[refs[0]], [refs[1]], [refs[2]], [refs[3], refs[4]]]
    s = [(refs[5], 0), (refs[7], 0), (refs[6], 0), (refs[8], 0)]
    xe = refs[9 : 9 + outer]
    held_t, held_f = refs[9 + outer : 11 + outer]
    sends = refs[11 + outer : 10 + 2 * outer]
    x, e, *scratch = refs[10 + 2 * outer :]
    dz = sub * INNER
    for k in range(outer):
        x[k * BLOCK : (k + 1) * BLOCK, :] = xe[k][:, :dz]
        e[k * BLOCK : (k + 1) * BLOCK, :] = xe[k][:, dz : dz + kv]
    parts = plane_parts(me_ref[0], w, s, scratch, outer, sub)
    for first, size, weight, factors in parts:
        base = dot(e[...], weight[...], 1, 1)
        for k in range(outer):
            extra = dot(xe[k][:, dz + kv :], factors[k][...], 1, 1)
            out = held_t if k == 0 else sends[k - 1]
            rows = slice(k * BLOCK, (k + 1) * BLOCK)
            out[:, pl.ds(first, size)] = (base[rows] + extra).astype(BF)
    step = 256
    for c in range(0, kv, step):
        part = sum(
            dot(x[:, pl.ds(first, size)], weight[:, c : c + step], 1, 0)
            for first, size, weight, _ in parts
        )
        held_f[:, c : c + step] = part[:BLOCK]
        for k in range(1, outer):
            rows = slice(k * BLOCK, (k + 1) * BLOCK)
            sends[k - 1][:, dz + c : dz + c + step] = part[rows].astype(BF)


def main_parts(me, wparts, sparts, xe, outer):
    sub, kv = wparts[0].shape
    rank = sparts[0].shape[-1]
    dz = sub * INNER
    return pl.pallas_call(
        lambda *refs: main_kernel(outer, sub, kv, *refs),
        out_shape=(
            jax.ShapeDtypeStruct((BLOCK, dz), BF),
            jax.ShapeDtypeStruct((BLOCK, kv), F32),
        )
        + tuple(jax.ShapeDtypeStruct((BLOCK, dz + kv), BF) for _ in range(outer - 1)),
        in_specs=[SM] + [VM] * (9 + outer),
        out_specs=(VM,) * (1 + outer),
        scratch_shapes=[
            pltpu.VMEM((outer * BLOCK, dz), BF),
            pltpu.VMEM((outer * BLOCK, kv), BF),
        ]
        + plane_scratch(outer, sub, kv, rank),
        compiler_params=params(48),
        cost_estimate=COST,
        name="plane_products",
    )(me, *wparts, *sparts, *xe)


def shrink_kernel(outer, sub, me_ref, *refs):
    s = [refs[0], refs[2], refs[1], refs[3]]
    xe = refs[4 : 4 + outer]
    outs = refs[4 + outer : 4 + 2 * outer]
    scratch = refs[4 + 2 * outer :]
    own = lax.rem(me_ref[0], INNER)
    for k in range(outer):
        total = None
        for j, ref in enumerate(s):
            first = pl.multiple_of(jnp.bitwise_xor(own, j) * sub, sub)
            if scratch:
                scratch[0][pl.ds(first, sub), :] = ref[k]
            else:
                term = dot(xe[k][:, pl.ds(first, sub)], ref[k], 1, 0)
                total = term if total is None else total + term
        if scratch:
            total = dot(xe[k][:, : sub * INNER], scratch[0][...], 1, 0)
        outs[k][...] = total


def shrink_parts(me, sparts, xe, outer):
    sub, rank = sparts[0].shape[1:]
    scratch = [] if sub % 128 == 0 else [pltpu.VMEM((sub * INNER, rank), BF)]
    return pl.pallas_call(
        lambda *refs: shrink_kernel(outer, sub, *refs),
        out_shape=tuple(jax.ShapeDtypeStruct((BLOCK, rank), F32) for _ in range(outer)),
        in_specs=[SM] + [VM] * (4 + outer),
        out_specs=(VM,) * outer,
        scratch_shapes=scratch,
        compiler_params=params(24),
        cost_estimate=COST,
        name="shrink_parts",
    )(me, *sparts, *xe)


def rows_kernel(outer, dz, me_ref, ids_ref, ranks_ref, *refs):
    parts = refs[:outer]
    up, own, extra, eg = refs[outer:]
    rank = ranks_ref[ids_ref[me_ref[0]]]
    low = sum(p[...] for p in parts)
    cols = lax.broadcasted_iota(jnp.int32, low.shape, 1)
    shrink = jnp.where(cols < rank, low, 0.0).astype(BF)
    scale = adapter_scale(rank)[:, :1]
    extra[...] = dot(shrink, up[...], 1, 0) * scale
    kv = up.shape[1]
    eg[...] = (dot(shrink, own[:, dz : dz + kv], 0, 0) * scale).astype(BF)


def shrunk_rows(me, ids, ranks, parts, up, own):
    rank_cap, kv = up.shape
    outer = len(parts)
    return pl.pallas_call(
        lambda *refs: rows_kernel(outer, own.shape[1] - kv - rank_cap, *refs),
        out_shape=(
            jax.ShapeDtypeStruct((BLOCK, kv), F32),
            jax.ShapeDtypeStruct((rank_cap, kv), BF),
        ),
        in_specs=[SM, SM, SM] + [VM] * (outer + 2),
        out_specs=(VM, VM),
        compiler_params=params(24),
        cost_estimate=COST,
        name="shrunk_rows",
    )(me, ids, ranks, *parts, up, own)


def pack_kernel(outer, sub, rank, me_ref, *refs):
    xe, outs = refs[:outer], refs[outer:]
    own = lax.rem(me_ref[0], INNER)
    last = xe[0].shape[1] - rank
    for j, out in enumerate(outs):
        for k in range(outer):
            out[k * BLOCK : (k + 1) * BLOCK, :rank] = xe[k][:, last:]
        for quarter in range(INNER):

            @pl.when(jnp.bitwise_xor(own, j) == quarter)
            def _(quarter=quarter, out=out):
                for k in range(outer):
                    part = xe[k][:, quarter * sub : (quarter + 1) * sub]
                    out[k * BLOCK : (k + 1) * BLOCK, rank:] = part


def pack(me, xe, sub, rank, outer):
    shape = jax.ShapeDtypeStruct((outer * BLOCK, rank + sub), BF)
    return pl.pallas_call(
        lambda *refs: pack_kernel(outer, sub, rank, *refs),
        out_shape=(shape,) * INNER,
        in_specs=[SM] + [VM] * outer,
        out_specs=(VM,) * INNER,
        compiler_params=params(24),
        cost_estimate=COST,
        name="pack_columns",
    )(me, *xe)


def down_kernel(per, blocks, rank, me_ref, ids_ref, *refs):
    out = refs[-1]
    first = pl.program_id(0) * per
    out[...] = jnp.zeros_like(out)

    for j, ref in enumerate(refs[:-1]):

        def each(k, carry, ref=ref, j=j):
            slot = ids_ref[jnp.bitwise_xor(me_ref[0], k * INNER + j)] - first

            @pl.when(jnp.logical_and(slot >= 0, slot < per))
            def _():
                rows = pl.ds(pl.multiple_of(k * BLOCK, BLOCK), BLOCK)
                out[slot] += dot(ref[rows, rank:], ref[rows, :rank], 0, 0)

            return carry

        lax.fori_loop(0, blocks, each, 0)


def down_grad(me, ids, packed, adapters, rank):
    shape = packed[0].shape
    sub = shape[1] - rank
    blocks = shape[0] // BLOCK
    per = 4
    whole = pl.BlockSpec(shape, lambda i, *_: (0, 0))
    return pl.pallas_call(
        lambda *refs: down_kernel(per, blocks, rank, *refs),
        grid_spec=pltpu.PrefetchScalarGridSpec(
            num_scalar_prefetch=2,
            grid=(adapters // per,),
            in_specs=[whole] * len(packed),
            out_specs=pl.BlockSpec((per, sub, rank), lambda i, *_: (i, 0, 0)),
        ),
        out_shape=jax.ShapeDtypeStruct((adapters, sub, rank), F32),
        compiler_params=params(32),
        cost_estimate=COST,
        name="down_gradient",
    )(me, ids, *packed)


def up_kernel(per, blocks, ids_ref, got, out):
    first = pl.program_id(0) * per
    out[...] = jnp.zeros_like(out)

    def each(i, carry):
        slot = ids_ref[i] - first

        @pl.when(jnp.logical_and(slot >= 0, slot < per))
        def _():
            out[slot] += got[i].astype(F32)

        return carry

    lax.fori_loop(0, blocks, each, 0)


def up_grad(ids, got, adapters):
    blocks, part, kv = got.shape
    per = 16
    return pl.pallas_call(
        lambda *refs: up_kernel(per, blocks, *refs),
        grid_spec=pltpu.PrefetchScalarGridSpec(
            num_scalar_prefetch=1,
            grid=(adapters // per,),
            in_specs=[pl.BlockSpec(got.shape, lambda i, *_: (0, 0, 0))],
            out_specs=pl.BlockSpec((per, part, kv), lambda i, *_: (i, 0, 0)),
        ),
        out_shape=jax.ShapeDtypeStruct((adapters, part, kv), F32),
        compiler_params=params(24),
        cost_estimate=COST,
        name="up_gradient",
    )(ids, got)


def join_kernel(outer, dz, me_ref, held_t, held_f, extra, *refs):
    got, proj, grad = refs[:-2], refs[-2], refs[-1]
    plane = lax.div(me_ref[0], INNER)
    for k in range(outer):
        at = pl.multiple_of(jnp.bitwise_xor(plane, k) * dz, dz)
        grad[:, pl.ds(at, dz)] = held_t[...] if k == 0 else got[k - 1][:, :dz]
    total = held_f[...] + extra[...] + sum(g[:, dz:].astype(F32) for g in got)
    proj[...] = total.astype(BF)


def join(me, held_t, held_f, extra, got):
    rows, dz = held_t.shape
    outer = 1 + len(got)
    return pl.pallas_call(
        lambda *refs: join_kernel(outer, dz, *refs),
        out_shape=(
            jax.ShapeDtypeStruct(held_f.shape, BF),
            jax.ShapeDtypeStruct((rows, dz * outer), BF),
        ),
        in_specs=[SM] + [VM] * (2 + outer),
        out_specs=(VM, VM),
        compiler_params=params(24),
        cost_estimate=COST,
        name="join_columns",
    )(me, held_t, held_f, extra, *got)


def build(devices):
    outer = devices // INNER

    def swap(value, mask):
        return lax.ppermute(value, "fsdp", [(i, i ^ mask) for i in range(devices)])

    def on_device(tokens, grad_out, base_weight, shrink_factor, expand_factor,
                  rank_per_adapter, block_adapter, block_rows):
        adapters, sub, rank = shrink_factor.shape
        kv = base_weight.shape[1]
        me = lax.axis_index("fsdp").reshape(1).astype(jnp.int32)

        def after(value, earlier):
            return lax.optimization_barrier((value, earlier))[0]

        def to_planes(parts):
            got = {k: swap(parts[k], k * INNER) for k in reversed(range(1, outer))}
            return [parts[0]] + [got[k] for k in range(1, outer)]

        up_send = jnp.take(expand_factor, block_adapter, axis=0, mode="clip")
        up = lax.all_to_all(up_send, "fsdp", split_axis=0, concat_axis=0, tiled=True)
        up = up.reshape(rank, kv)

        s_send, s_keep = pick(me, after(block_adapter, up_send), shrink_factor, outer)
        s_x = swap(after(s_send, up), 2)
        w_x = swap(after(base_weight, up), 2)
        s_c = swap(s_keep[outer:], 1)
        s_xc = swap(s_x[outer:], 1)
        w_c = swap(base_weight, 1)
        w_xc = [swap(w_x[: sub // 2], 1), swap(w_x[sub // 2 :], 1)]
        wparts = (base_weight, w_c, w_x, *w_xc)
        sparts = (s_keep, s_x, s_c, s_xc)

        cuts = first_sends(
            me, block_adapter, rank_per_adapter, block_rows, tokens, grad_out,
            after(up, s_keep), outer,
        )
        xe = to_planes(cuts)

        low = shrink_parts(me, sparts, xe, outer)
        held_t, held_f, *sends = main_parts(me, wparts, sparts, after(xe, low), outer)
        low = to_planes(low)
        extra, eg = shrunk_rows(
            me, block_adapter, rank_per_adapter, after(low, sends), up, cuts[0]
        )
        eg_got = eg.reshape(devices, rank // devices, kv)
        eg_got = lax.all_to_all(eg_got, "fsdp", split_axis=0, concat_axis=0, tiled=True)

        packed = pack(me, after(xe, eg), sub, rank, outer)
        packed = [p if j == 0 else swap(p, j) for j, p in enumerate(packed)]
        shrink_grad = down_grad(me, block_adapter, packed, adapters, rank)
        expand_grad = up_grad(after(block_adapter, shrink_grad), eg_got, adapters)
        got = to_planes([held_t] + sends)[1:]
        projected, token_input_gradient = join(
            me, held_t, held_f, extra, after(got, expand_grad)
        )
        return (projected, token_input_gradient, shrink_grad, expand_grad)

    return on_device


def solution(mesh):
    placed = (
        P(("groups", "fsdp"), None),
        P(("groups", "fsdp"), None),
        P("fsdp", None),
        P("groups", "fsdp", None),
        P("groups", "fsdp", None),
        P("groups"),
        P("groups"),
        P(("groups", "fsdp")),
    )
    return jax.shard_map(
        build(mesh.shape["fsdp"]),
        mesh=mesh,
        in_specs=placed,
        out_specs=(
            P(("groups", "fsdp"), None),
            P(("groups", "fsdp"), None),
            P("groups", "fsdp", None),
            P("groups", "fsdp", None),
        ),
        check_vma=False,
    )
```

```python
import jax
import jax.numpy as jnp
from jax import lax
from jax.experimental import pallas as pl
from jax.experimental.pallas import tpu as pltpu
from jax.sharding import PartitionSpec as P

BLOCK = 128
ADAPTER_STRENGTH = 16.0
INNER = 4
MIB = 1 << 20
BF = jnp.bfloat16
F32 = jnp.float32

HBM = pl.BlockSpec(memory_space=pltpu.HBM)
VM = pl.BlockSpec(memory_space=pltpu.VMEM)
SM = pl.BlockSpec(memory_space=pltpu.SMEM)


def params(mib):
    return pltpu.CompilerParams(vmem_limit_bytes=mib * MIB)


COST = pl.CostEstimate(flops=1, bytes_accessed=1, transcendentals=0)


def dot(a, b, ca, cb):
    return lax.dot_general(a, b, (((ca,), (cb,)), ((), ())), preferred_element_type=F32)


def adapter_scale(rank):
    return ADAPTER_STRENGTH / jnp.sqrt(jnp.full((BLOCK, BLOCK), rank, jnp.int32).astype(F32))


def pick_kernel(outer, me_ref, ids_ref, factor, s_send, s_keep, sem):
    def start(i, carry):
        core = lax.div(i, outer)
        own = jnp.bitwise_xor(me_ref[0], lax.rem(i, outer) * INNER + core)
        pltpu.make_async_copy(factor.at[ids_ref[own]], s_keep.at[i], sem.at[0]).start()
        far = jnp.bitwise_xor(own, 2)
        pltpu.make_async_copy(factor.at[ids_ref[far]], s_send.at[i], sem.at[1]).start()
        return carry

    half = s_keep.shape[0]
    lax.fori_loop(0, half, start, 0)
    pltpu.make_async_copy(factor.at[pl.ds(0, half)], s_keep, sem.at[0]).wait()
    pltpu.make_async_copy(factor.at[pl.ds(0, half)], s_send, sem.at[1]).wait()


def pick(me, ids, factor, outer):
    picked = jax.ShapeDtypeStruct((2 * outer,) + factor.shape[1:], BF)
    return pl.pallas_call(
        lambda *refs: pick_kernel(outer, *refs),
        out_shape=(picked, picked),
        in_specs=[SM, SM, HBM],
        out_specs=(VM, VM),
        scratch_shapes=[pltpu.SemaphoreType.DMA((2,))],
        compiler_params=params(57),
        cost_estimate=COST,
        name="pick_factors",
    )(me, ids, factor)


def mask_kernel(rows_ref, grad, out):
    rows = lax.broadcasted_iota(jnp.int32, grad.shape, 0)
    out[...] = jnp.where(rows < rows_ref[0], grad[...].astype(F32), 0.0).astype(BF)


def mask_rows(block_rows, grad):
    return pl.pallas_call(
        mask_kernel,
        out_shape=jax.ShapeDtypeStruct(grad.shape, BF),
        in_specs=[SM, VM],
        out_specs=VM,
        compiler_params=params(8),
        cost_estimate=COST,
        name="mask_rows",
    )(block_rows, grad)


def first_kernel(outer, me_ref, ids_ref, ranks_ref, tokens, up_ref, *refs):
    grads, outs = refs[:-outer], refs[-outer:]
    rank = ranks_ref[ids_ref[me_ref[0]]]
    plane = lax.div(me_ref[0], INNER)
    dz = tokens.shape[1] // outer
    rank_cap, kv = up_ref.shape
    back = dot(grads[0][...], up_ref[...], 1, 1) * adapter_scale(rank)
    cols = lax.broadcasted_iota(jnp.int32, back.shape, 1)
    back = jnp.where(cols < rank, back, 0.0).astype(BF)
    for k, out in enumerate(outs):
        at = pl.multiple_of(jnp.bitwise_xor(plane, k) * dz, dz)
        out[:, :dz] = tokens[:, pl.ds(at, dz)]
        out[:, dz : dz + rank_cap] = back
    at = dz + rank_cap
    for g in grads:
        for row in range(0, g.shape[0], BLOCK):
            outs[1][:, at : at + kv] = g[row : row + BLOCK, :]
            at += kv


def first_sends(me, ids, ranks, tokens, up, grads, outer):
    rows, width = tokens.shape
    rank_cap, kv = up.shape
    wide = width // outer + rank_cap
    more = outer // 2 * kv
    return pl.pallas_call(
        lambda *refs: first_kernel(outer, *refs),
        out_shape=tuple(
            jax.ShapeDtypeStruct((rows, wide + (more if k == 1 else 0)), BF)
            for k in range(outer)
        ),
        in_specs=[SM] * 3 + [VM] * (2 + len(grads)),
        out_specs=(VM,) * outer,
        compiler_params=params(32),
        cost_estimate=COST,
        name="first_sends",
    )(me, ids, ranks, tokens, up, *grads)


def plane_parts(me, w, s, scratch, outer, sub):
    own = lax.rem(me, INNER)
    parts = []
    for j, (ws, (ref, at)) in enumerate(zip(w, s)):
        first = pl.multiple_of(jnp.bitwise_xor(own, j) * sub, sub)
        row = 0
        for weight in ws:
            size = weight.shape[0]
            rows = slice(row, row + size)
            if scratch:
                wz, sz = scratch
                base = pl.multiple_of(first + row, size)
                wz[pl.ds(base, size), :] = weight[...]
                for k in range(outer):
                    sz[k, pl.ds(base, size), :] = ref[at + k, rows, :]
            else:
                base = pl.multiple_of(first + row, size)
                factors = [ref.at[at + k, rows] for k in range(outer)]
                parts.append((base, size, weight, factors))
            row += size
    if scratch:
        wz, sz = scratch
        parts = [(0, wz.shape[0], wz, [sz.at[k] for k in range(outer)])]
    return parts


def plane_scratch(outer, sub, kv, rank):
    if sub % 256 == 0:
        return []
    dz = sub * INNER
    return [pltpu.VMEM((dz, kv), BF), pltpu.VMEM((outer, dz, rank), BF)]


def main_kernel(evens, outer, sub, kv, me_ref, *refs):
    w = [[refs[0]], [refs[1]], [refs[2]], [refs[3], refs[4]]]
    s = [(refs[5], 0), (refs[7], 0), (refs[6], 0), (refs[8], 0)]
    rank = refs[5].shape[2]
    *ins, x, e = refs[9 : len(refs) - (0 if sub % 256 == 0 else 2)]
    scratch = refs[9 + len(ins) + 2 :]
    n_outs = 1 + outer + outer // 2
    ins, outs = ins[:-n_outs], ins[-n_outs:]
    held_t, *sends = outs[:outer]
    held_f = outs[outer]
    even_f = outs[outer + 1 : outer + outer // 2]
    odd_f = outs[outer + outer // 2 :]
    xe, grads = ins[:outer], ins[outer:]
    dz = sub * INNER
    for k in range(outer):
        x[k * BLOCK : (k + 1) * BLOCK, :] = xe[k][:, :dz]
    at = 0
    for g in grads:
        for row in range(0, g.shape[0], BLOCK):
            k = evens[at]
            e[k * BLOCK : (k + 1) * BLOCK, :] = g[row : row + BLOCK, :]
            first = dz + rank + at * kv
            k = k ^ 1
            e[k * BLOCK : (k + 1) * BLOCK, :] = xe[1][:, first : first + kv]
            at += 1
    parts = plane_parts(me_ref[0], w, s, scratch, outer, sub)
    for first, size, weight, factors in parts:
        base = dot(e[...], weight[...], 1, 1)
        for k in range(outer):
            extra = dot(xe[k][:, dz : dz + rank], factors[k][...], 1, 1)
            out = held_t if k == 0 else sends[k - 1]
            rows = slice(k * BLOCK, (k + 1) * BLOCK)
            out[:, pl.ds(first, size)] = (base[rows] + extra).astype(BF)
    step = 256
    for c in range(0, kv, step):
        part = sum(
            dot(x[:, pl.ds(first, size)], weight[:, c : c + step], 1, 0)
            for first, size, weight, _ in parts
        )
        for k in range(outer):
            value = part[k * BLOCK : (k + 1) * BLOCK]
            cols = slice(c, c + step)
            if k == 0:
                held_f[:, cols] = value
            elif k == 1:
                sends[0][:, dz + c : dz + c + step] = value.astype(BF)
            elif k % 2 == 0:
                even_f[k // 2 - 1][:, cols] = value
            else:
                row = (k // 2 - 1) * BLOCK
                odd_f[0][row : row + BLOCK, cols] = value.astype(BF)


def main_parts(me, wparts, sparts, xe, grads, evens, outer):
    sub, kv = wparts[0].shape
    rank = sparts[0].shape[-1]
    dz = sub * INNER
    half = outer // 2
    return pl.pallas_call(
        lambda *refs: main_kernel(evens, outer, sub, kv, *refs),
        out_shape=(
            jax.ShapeDtypeStruct((BLOCK, dz), BF),
            jax.ShapeDtypeStruct((BLOCK, dz + kv), BF),
        )
        + (jax.ShapeDtypeStruct((BLOCK, dz), BF),) * (outer - 2)
        + (jax.ShapeDtypeStruct((BLOCK, kv), F32),) * half
        + (jax.ShapeDtypeStruct(((half - 1) * BLOCK, kv), BF),),
        in_specs=[SM] + [VM] * (9 + outer + len(grads)),
        out_specs=(VM,) * (1 + outer + half),
        scratch_shapes=[
            pltpu.VMEM((outer * BLOCK, dz), BF),
            pltpu.VMEM((outer * BLOCK, kv), BF),
        ]
        + plane_scratch(outer, sub, kv, rank),
        compiler_params=params(48),
        cost_estimate=COST,
        name="plane_products",
    )(me, *wparts, *sparts, *xe, *grads)


def shrink_kernel(outer, sub, me_ref, *refs):
    s = [refs[0], refs[2], refs[1], refs[3]]
    xe = refs[4 : 4 + outer]
    outs = refs[4 + outer : 4 + 2 * outer]
    scratch = refs[4 + 2 * outer :]
    own = lax.rem(me_ref[0], INNER)
    for k in range(outer):
        total = None
        for j, ref in enumerate(s):
            first = pl.multiple_of(jnp.bitwise_xor(own, j) * sub, sub)
            if scratch:
                scratch[0][pl.ds(first, sub), :] = ref[k]
            else:
                term = dot(xe[k][:, pl.ds(first, sub)], ref[k], 1, 0)
                total = term if total is None else total + term
        if scratch:
            total = dot(xe[k][:, : sub * INNER], scratch[0][...], 1, 0)
        outs[k][...] = total


def shrink_parts(me, sparts, xe, outer):
    sub, rank = sparts[0].shape[1:]
    scratch = [] if sub % 128 == 0 else [pltpu.VMEM((sub * INNER, rank), BF)]
    return pl.pallas_call(
        lambda *refs: shrink_kernel(outer, sub, *refs),
        out_shape=tuple(jax.ShapeDtypeStruct((BLOCK, rank), F32) for _ in range(outer)),
        in_specs=[SM] + [VM] * (4 + outer),
        out_specs=(VM,) * outer,
        scratch_shapes=scratch,
        compiler_params=params(24),
        cost_estimate=COST,
        name="shrink_parts",
    )(me, *sparts, *xe)


def rows_kernel(outer, me_ref, ids_ref, ranks_ref, *refs):
    parts = refs[:outer]
    up, own, extra, eg = refs[outer:]
    rank = ranks_ref[ids_ref[me_ref[0]]]
    low = sum(p[...] for p in parts)
    cols = lax.broadcasted_iota(jnp.int32, low.shape, 1)
    shrink = jnp.where(cols < rank, low, 0.0).astype(BF)
    scale = adapter_scale(rank)[:, :1]
    extra[...] = dot(shrink, up[...], 1, 0) * scale
    eg[...] = (dot(shrink, own[...], 0, 0) * scale).astype(BF)


def shrunk_rows(me, ids, ranks, parts, up, own):
    rank_cap, kv = up.shape
    outer = len(parts)
    return pl.pallas_call(
        lambda *refs: rows_kernel(outer, *refs),
        out_shape=(
            jax.ShapeDtypeStruct((BLOCK, kv), F32),
            jax.ShapeDtypeStruct((rank_cap, kv), BF),
        ),
        in_specs=[SM, SM, SM] + [VM] * (outer + 2),
        out_specs=(VM, VM),
        compiler_params=params(24),
        cost_estimate=COST,
        name="shrunk_rows",
    )(me, ids, ranks, *parts, up, own)


def pack_kernel(outer, sub, rank, me_ref, *refs):
    xe, outs = refs[:outer], refs[outer:]
    own = lax.rem(me_ref[0], INNER)
    last = sub * INNER
    for j, out in enumerate(outs):
        for k in range(outer):
            out[k * BLOCK : (k + 1) * BLOCK, :rank] = xe[k][:, last : last + rank]
        for quarter in range(INNER):

            @pl.when(jnp.bitwise_xor(own, j) == quarter)
            def _(quarter=quarter, out=out):
                for k in range(outer):
                    part = xe[k][:, quarter * sub : (quarter + 1) * sub]
                    out[k * BLOCK : (k + 1) * BLOCK, rank:] = part


def pack(me, xe, sub, rank, outer):
    shape = jax.ShapeDtypeStruct((outer * BLOCK, rank + sub), BF)
    return pl.pallas_call(
        lambda *refs: pack_kernel(outer, sub, rank, *refs),
        out_shape=(shape,) * INNER,
        in_specs=[SM] + [VM] * outer,
        out_specs=(VM,) * INNER,
        compiler_params=params(24),
        cost_estimate=COST,
        name="pack_columns",
    )(me, *xe)


def down_kernel(per, blocks, rank, me_ref, ids_ref, *refs):
    out = refs[-1]
    first = pl.program_id(0) * per
    out[...] = jnp.zeros_like(out)

    for j, ref in enumerate(refs[:-1]):

        def each(k, carry, ref=ref, j=j):
            slot = ids_ref[jnp.bitwise_xor(me_ref[0], k * INNER + j)] - first

            @pl.when(jnp.logical_and(slot >= 0, slot < per))
            def _():
                rows = pl.ds(pl.multiple_of(k * BLOCK, BLOCK), BLOCK)
                out[slot] += dot(ref[rows, rank:], ref[rows, :rank], 0, 0)

            return carry

        lax.fori_loop(0, blocks, each, 0)


def down_grad(me, ids, packed, adapters, rank):
    shape = packed[0].shape
    sub = shape[1] - rank
    blocks = shape[0] // BLOCK
    per = 4
    whole = pl.BlockSpec(shape, lambda i, *_: (0, 0))
    return pl.pallas_call(
        lambda *refs: down_kernel(per, blocks, rank, *refs),
        grid_spec=pltpu.PrefetchScalarGridSpec(
            num_scalar_prefetch=2,
            grid=(adapters // per,),
            in_specs=[whole] * len(packed),
            out_specs=pl.BlockSpec((per, sub, rank), lambda i, *_: (i, 0, 0)),
        ),
        out_shape=jax.ShapeDtypeStruct((adapters, sub, rank), F32),
        compiler_params=params(32),
        cost_estimate=COST,
        name="down_gradient",
    )(me, ids, *packed)


def up_kernel(per, blocks, ids_ref, got, out):
    first = pl.program_id(0) * per
    out[...] = jnp.zeros_like(out)

    def each(i, carry):
        slot = ids_ref[i] - first

        @pl.when(jnp.logical_and(slot >= 0, slot < per))
        def _():
            out[slot] += got[i].astype(F32)

        return carry

    lax.fori_loop(0, blocks, each, 0)


def up_grad(ids, got, adapters):
    blocks, part, kv = got.shape
    per = 16
    return pl.pallas_call(
        lambda *refs: up_kernel(per, blocks, *refs),
        grid_spec=pltpu.PrefetchScalarGridSpec(
            num_scalar_prefetch=1,
            grid=(adapters // per,),
            in_specs=[pl.BlockSpec(got.shape, lambda i, *_: (0, 0, 0))],
            out_specs=pl.BlockSpec((per, part, kv), lambda i, *_: (i, 0, 0)),
        ),
        out_shape=jax.ShapeDtypeStruct((adapters, part, kv), F32),
        compiler_params=params(24),
        cost_estimate=COST,
        name="up_gradient",
    )(ids, got)


def join_kernel(outer, dz, me_ref, held_t, held_f, extra, *refs):
    got, parts, (proj, grad) = refs[: outer - 1], refs[outer - 1 : -2], refs[-2:]
    plane = lax.div(me_ref[0], INNER)
    for k in range(outer):
        at = pl.multiple_of(jnp.bitwise_xor(plane, k) * dz, dz)
        grad[:, pl.ds(at, dz)] = held_t[...] if k == 0 else got[k - 1][:, :dz]
    total = held_f[...] + extra[...] + got[0][:, dz:].astype(F32)
    proj[...] = (total + sum(p[...].astype(F32) for p in parts)).astype(BF)


def join(me, held_t, held_f, extra, got, parts):
    rows, dz = held_t.shape
    outer = 1 + len(got)
    return pl.pallas_call(
        lambda *refs: join_kernel(outer, dz, *refs),
        out_shape=(
            jax.ShapeDtypeStruct(held_f.shape, BF),
            jax.ShapeDtypeStruct((rows, dz * outer), BF),
        ),
        in_specs=[SM] + [VM] * (2 + outer + len(parts)),
        out_specs=(VM, VM),
        compiler_params=params(24),
        cost_estimate=COST,
        name="join_columns",
    )(me, held_t, held_f, extra, *got, *parts)


def build(devices):
    outer = devices // INNER

    def swap(value, mask):
        return lax.ppermute(value, "fsdp", [(i, i ^ mask) for i in range(devices)])

    def on_device(tokens, grad_out, base_weight, shrink_factor, expand_factor,
                  rank_per_adapter, block_adapter, block_rows):
        adapters, sub, rank = shrink_factor.shape
        kv = base_weight.shape[1]
        me = lax.axis_index("fsdp").reshape(1).astype(jnp.int32)

        def after(value, earlier):
            return lax.optimization_barrier((value, earlier))[0]

        def to_planes(parts):
            got = {k: swap(parts[k], k * INNER) for k in range(1, outer)}
            return [parts[0]] + [got[k] for k in range(1, outer)]

        masked = mask_rows(block_rows, grad_out)
        grads, evens = [masked], [0]
        step = outer // 2
        while step > 1:
            stack = grads[0] if len(grads) == 1 else jnp.concatenate(grads, axis=0)
            grads.append(swap(stack, step * INNER))
            evens = evens + [k ^ step for k in evens]
            step //= 2

        up_send = jnp.take(expand_factor, after(block_adapter, masked), axis=0, mode="clip")
        up = lax.all_to_all(up_send, "fsdp", split_axis=0, concat_axis=0, tiled=True)
        up = up.reshape(rank, kv)

        s_send, s_keep = pick(me, after(block_adapter, up_send), shrink_factor, outer)
        s_x = swap(after(s_send, (up, grads)), 2)
        w_x = swap(after(base_weight, (up, grads, s_keep)), 2)
        s_c = swap(after(s_keep, s_x)[outer:], 1)
        s_xc = swap(s_x[outer:], 1)
        w_c = swap(after(base_weight, w_x), 1)
        w_xc = [swap(w_x[: sub // 2], 1), swap(w_x[sub // 2 :], 1)]
        wparts = (base_weight, w_c, w_x, *w_xc)
        sparts = (s_keep, s_x, s_c, s_xc)

        cuts = first_sends(
            me, block_adapter, rank_per_adapter, tokens, after(up, s_keep), grads, outer
        )
        xe = to_planes(cuts)

        low = shrink_parts(me, sparts, xe, outer)
        products = main_parts(
            me, wparts, sparts, after(xe, low), grads, evens, outer
        )
        sends, held_f = products[:outer], products[outer]
        even_f, odd_f = products[outer + 1 : -1], products[-1]
        odd_got = swap(odd_f, INNER)
        low = to_planes(low)
        extra, eg = shrunk_rows(
            me, block_adapter, rank_per_adapter, after(low, products), up, masked
        )
        eg_got = eg.reshape(devices, rank // devices, kv)
        eg_got = lax.all_to_all(eg_got, "fsdp", split_axis=0, concat_axis=0, tiled=True)

        packed = pack(me, after(xe, eg), sub, rank, outer)
        packed = [p if j == 0 else swap(p, j) for j, p in enumerate(packed)]
        shrink_grad = down_grad(me, block_adapter, packed, adapters, rank)
        expand_grad = up_grad(after(block_adapter, shrink_grad), eg_got, adapters)
        parts = []
        for i, value in enumerate(even_f):
            value = value + odd_got[i * BLOCK : (i + 1) * BLOCK].astype(F32)
            parts.append(swap(value.astype(BF), 2 * (i + 1) * INNER))
        held_t, *got = to_planes(sends)
        projected, token_input_gradient = join(
            me, held_t, held_f, extra, after(got, expand_grad), parts
        )
        return (projected, token_input_gradient, shrink_grad, expand_grad)

    return on_device


def solution(mesh):
    placed = (
        P(("groups", "fsdp"), None),
        P(("groups", "fsdp"), None),
        P("fsdp", None),
        P("groups", "fsdp", None),
        P("groups", "fsdp", None),
        P("groups"),
        P("groups"),
        P(("groups", "fsdp")),
    )
    return jax.shard_map(
        build(mesh.shape["fsdp"]),
        mesh=mesh,
        in_specs=placed,
        out_specs=(
            P(("groups", "fsdp"), None),
            P(("groups", "fsdp"), None),
            P("groups", "fsdp", None),
            P("groups", "fsdp", None),
        ),
        check_vma=False,
    )
```

```python
import jax
import jax.numpy as jnp
from jax import lax
from jax.experimental import pallas as pl
from jax.experimental.pallas import tpu as pltpu
from jax.sharding import PartitionSpec as P

BLOCK = 128
ADAPTER_STRENGTH = 16.0
INNER = 4
MIB = 1 << 20
BF = jnp.bfloat16
F32 = jnp.float32

HBM = pl.BlockSpec(memory_space=pltpu.HBM)
VM = pl.BlockSpec(memory_space=pltpu.VMEM)
SM = pl.BlockSpec(memory_space=pltpu.SMEM)


def params(mib):
    return pltpu.CompilerParams(vmem_limit_bytes=mib * MIB)


COST = pl.CostEstimate(flops=1, bytes_accessed=1, transcendentals=0)


def dot(a, b, ca, cb):
    return lax.dot_general(a, b, (((ca,), (cb,)), ((), ())), preferred_element_type=F32)


def adapter_scale(rank):
    return ADAPTER_STRENGTH / jnp.sqrt(jnp.full((BLOCK, BLOCK), rank, jnp.int32).astype(F32))


def pick_kernel(outer, me_ref, ids_ref, factor, s_send, s_keep, sem):
    def start(i, carry):
        core = lax.div(i, outer)
        own = jnp.bitwise_xor(me_ref[0], lax.rem(i, outer) * INNER + core)
        pltpu.make_async_copy(factor.at[ids_ref[own]], s_keep.at[i], sem.at[0]).start()
        far = jnp.bitwise_xor(own, 2)
        pltpu.make_async_copy(factor.at[ids_ref[far]], s_send.at[i], sem.at[1]).start()
        return carry

    half = s_keep.shape[0]
    lax.fori_loop(0, half, start, 0)
    pltpu.make_async_copy(factor.at[pl.ds(0, half)], s_keep, sem.at[0]).wait()
    pltpu.make_async_copy(factor.at[pl.ds(0, half)], s_send, sem.at[1]).wait()


def pick(me, ids, factor, outer):
    picked = jax.ShapeDtypeStruct((2 * outer,) + factor.shape[1:], BF)
    return pl.pallas_call(
        lambda *refs: pick_kernel(outer, *refs),
        out_shape=(picked, picked),
        in_specs=[SM, SM, HBM],
        out_specs=(VM, VM),
        scratch_shapes=[pltpu.SemaphoreType.DMA((2,))],
        compiler_params=params(57),
        cost_estimate=COST,
        name="pick_factors",
    )(me, ids, factor)


def mask_kernel(rows_ref, grad, out):
    rows = lax.broadcasted_iota(jnp.int32, grad.shape, 0)
    out[...] = jnp.where(rows < rows_ref[0], grad[...].astype(F32), 0.0).astype(BF)


def mask_rows(block_rows, grad):
    return pl.pallas_call(
        mask_kernel,
        out_shape=jax.ShapeDtypeStruct(grad.shape, BF),
        in_specs=[SM, VM],
        out_specs=VM,
        compiler_params=params(8),
        cost_estimate=COST,
        name="mask_rows",
    )(block_rows, grad)


def first_kernel(outer, me_ref, ids_ref, ranks_ref, tokens, up_ref, *refs):
    grads, outs = refs[:-outer], refs[-outer:]
    rank = ranks_ref[ids_ref[me_ref[0]]]
    plane = lax.div(me_ref[0], INNER)
    dz = tokens.shape[1] // outer
    rank_cap, kv = up_ref.shape
    back = dot(grads[0][...], up_ref[...], 1, 1) * adapter_scale(rank)
    cols = lax.broadcasted_iota(jnp.int32, back.shape, 1)
    back = jnp.where(cols < rank, back, 0.0).astype(BF)
    for k, out in enumerate(outs):
        at = pl.multiple_of(jnp.bitwise_xor(plane, k) * dz, dz)
        out[:, :dz] = tokens[:, pl.ds(at, dz)]
        out[:, dz : dz + rank_cap] = back
    at = dz + rank_cap
    for g in grads:
        for row in range(0, g.shape[0], BLOCK):
            outs[1][:, at : at + kv] = g[row : row + BLOCK, :]
            at += kv


def first_sends(me, ids, ranks, tokens, up, grads, outer):
    rows, width = tokens.shape
    rank_cap, kv = up.shape
    wide = width // outer + rank_cap
    more = outer // 2 * kv
    return pl.pallas_call(
        lambda *refs: first_kernel(outer, *refs),
        out_shape=tuple(
            jax.ShapeDtypeStruct((rows, wide + (more if k == 1 else 0)), BF)
            for k in range(outer)
        ),
        in_specs=[SM] * 3 + [VM] * (2 + len(grads)),
        out_specs=(VM,) * outer,
        compiler_params=params(32),
        cost_estimate=COST,
        name="first_sends",
    )(me, ids, ranks, tokens, up, *grads)


def plane_parts(me, w, s, scratch, outer, sub):
    own = lax.rem(me, INNER)
    parts = []
    for j, (ws, (ref, at)) in enumerate(zip(w, s)):
        first = pl.multiple_of(jnp.bitwise_xor(own, j) * sub, sub)
        row = 0
        for weight in ws:
            size = weight.shape[0]
            rows = slice(row, row + size)
            if scratch:
                wz, sz = scratch
                base = pl.multiple_of(first + row, size)
                wz[pl.ds(base, size), :] = weight[...]
                for k in range(outer):
                    sz[k, pl.ds(base, size), :] = ref[at + k, rows, :]
            else:
                base = pl.multiple_of(first + row, size)
                factors = [ref.at[at + k, rows] for k in range(outer)]
                parts.append((base, size, weight, factors))
            row += size
    if scratch:
        wz, sz = scratch
        parts = [(0, wz.shape[0], wz, [sz.at[k] for k in range(outer)])]
    return parts


def plane_scratch(outer, sub, kv, rank):
    if sub % 256 == 0:
        return []
    dz = sub * INNER
    return [pltpu.VMEM((dz, kv), BF), pltpu.VMEM((outer, dz, rank), BF)]


def main_kernel(evens, outer, sub, kv, me_ref, *refs):
    w = [[refs[0]], [refs[1]], [refs[2]], [refs[3], refs[4]]]
    s = [(refs[5], 0), (refs[7], 0), (refs[6], 0), (refs[8], 0)]
    rank = refs[5].shape[2]
    *ins, x, e = refs[9 : len(refs) - (0 if sub % 256 == 0 else 2)]
    scratch = refs[9 + len(ins) + 2 :]
    n_outs = 1 + outer + outer // 2
    ins, outs = ins[:-n_outs], ins[-n_outs:]
    held_t, *sends = outs[:outer]
    held_f = outs[outer]
    even_f = outs[outer + 1 : outer + outer // 2]
    odd_f = outs[outer + outer // 2 :]
    xe, grads = ins[:outer], ins[outer:]
    dz = sub * INNER
    for k in range(outer):
        x[k * BLOCK : (k + 1) * BLOCK, :] = xe[k][:, :dz]
    at = 0
    for g in grads:
        for row in range(0, g.shape[0], BLOCK):
            k = evens[at]
            e[k * BLOCK : (k + 1) * BLOCK, :] = g[row : row + BLOCK, :]
            first = dz + rank + at * kv
            k = k ^ 1
            e[k * BLOCK : (k + 1) * BLOCK, :] = xe[1][:, first : first + kv]
            at += 1
    parts = plane_parts(me_ref[0], w, s, scratch, outer, sub)
    for first, size, weight, factors in parts:
        base = dot(e[...], weight[...], 1, 1)
        for k in range(outer):
            extra = dot(xe[k][:, dz : dz + rank], factors[k][...], 1, 1)
            out = held_t if k == 0 else sends[k - 1]
            rows = slice(k * BLOCK, (k + 1) * BLOCK)
            out[:, pl.ds(first, size)] = (base[rows] + extra).astype(BF)
    step = 256
    for c in range(0, kv, step):
        part = sum(
            dot(x[:, pl.ds(first, size)], weight[:, c : c + step], 1, 0)
            for first, size, weight, _ in parts
        )
        for k in range(outer):
            value = part[k * BLOCK : (k + 1) * BLOCK]
            cols = slice(c, c + step)
            if k == 0:
                held_f[:, cols] = value
            elif k == 1:
                sends[0][:, dz + c : dz + c + step] = value.astype(BF)
            elif k % 2 == 0:
                even_f[k // 2 - 1][:, cols] = value
            else:
                row = (k // 2 - 1) * BLOCK
                odd_f[0][row : row + BLOCK, cols] = value.astype(BF)


def main_parts(me, wparts, sparts, xe, grads, evens, outer):
    sub, kv = wparts[0].shape
    rank = sparts[0].shape[-1]
    dz = sub * INNER
    half = outer // 2
    return pl.pallas_call(
        lambda *refs: main_kernel(evens, outer, sub, kv, *refs),
        out_shape=(
            jax.ShapeDtypeStruct((BLOCK, dz), BF),
            jax.ShapeDtypeStruct((BLOCK, dz + kv), BF),
        )
        + (jax.ShapeDtypeStruct((BLOCK, dz), BF),) * (outer - 2)
        + (jax.ShapeDtypeStruct((BLOCK, kv), F32),) * half
        + (jax.ShapeDtypeStruct(((half - 1) * BLOCK, kv), BF),),
        in_specs=[SM] + [VM] * (9 + outer + len(grads)),
        out_specs=(VM,) * (1 + outer + half),
        scratch_shapes=[
            pltpu.VMEM((outer * BLOCK, dz), BF),
            pltpu.VMEM((outer * BLOCK, kv), BF),
        ]
        + plane_scratch(outer, sub, kv, rank),
        compiler_params=params(48),
        cost_estimate=COST,
        name="plane_products",
    )(me, *wparts, *sparts, *xe, *grads)


def shrink_kernel(outer, sub, me_ref, *refs):
    s = [refs[0], refs[2], refs[1], refs[3]]
    xe = refs[4 : 4 + outer]
    outs = refs[4 + outer : 4 + 2 * outer]
    scratch = refs[4 + 2 * outer :]
    own = lax.rem(me_ref[0], INNER)
    for k in range(outer):
        total = None
        for j, ref in enumerate(s):
            first = pl.multiple_of(jnp.bitwise_xor(own, j) * sub, sub)
            if scratch:
                scratch[0][pl.ds(first, sub), :] = ref[k]
            else:
                term = dot(xe[k][:, pl.ds(first, sub)], ref[k], 1, 0)
                total = term if total is None else total + term
        if scratch:
            total = dot(xe[k][:, : sub * INNER], scratch[0][...], 1, 0)
        outs[k][...] = total


def shrink_parts(me, sparts, xe, outer):
    sub, rank = sparts[0].shape[1:]
    scratch = [] if sub % 128 == 0 else [pltpu.VMEM((sub * INNER, rank), BF)]
    return pl.pallas_call(
        lambda *refs: shrink_kernel(outer, sub, *refs),
        out_shape=tuple(jax.ShapeDtypeStruct((BLOCK, rank), F32) for _ in range(outer)),
        in_specs=[SM] + [VM] * (4 + outer),
        out_specs=(VM,) * outer,
        scratch_shapes=scratch,
        compiler_params=params(24),
        cost_estimate=COST,
        name="shrink_parts",
    )(me, *sparts, *xe)


def rows_kernel(outer, me_ref, ids_ref, ranks_ref, *refs):
    parts = refs[:outer]
    up, own, extra, eg = refs[outer:]
    rank = ranks_ref[ids_ref[me_ref[0]]]
    low = sum(p[...] for p in parts)
    cols = lax.broadcasted_iota(jnp.int32, low.shape, 1)
    shrink = jnp.where(cols < rank, low, 0.0).astype(BF)
    scale = adapter_scale(rank)[:, :1]
    extra[...] = dot(shrink, up[...], 1, 0) * scale
    eg[...] = (dot(shrink, own[...], 0, 0) * scale).astype(BF)


def shrunk_rows(me, ids, ranks, parts, up, own):
    rank_cap, kv = up.shape
    outer = len(parts)
    return pl.pallas_call(
        lambda *refs: rows_kernel(outer, *refs),
        out_shape=(
            jax.ShapeDtypeStruct((BLOCK, kv), F32),
            jax.ShapeDtypeStruct((rank_cap, kv), BF),
        ),
        in_specs=[SM, SM, SM] + [VM] * (outer + 2),
        out_specs=(VM, VM),
        compiler_params=params(24),
        cost_estimate=COST,
        name="shrunk_rows",
    )(me, ids, ranks, *parts, up, own)


def pack_kernel(outer, sub, rank, me_ref, *refs):
    xe, outs = refs[:outer], refs[outer:]
    own = lax.rem(me_ref[0], INNER)
    last = sub * INNER
    for j, out in enumerate(outs):
        for k in range(outer):
            out[k * BLOCK : (k + 1) * BLOCK, :rank] = xe[k][:, last : last + rank]
        for quarter in range(INNER):

            @pl.when(jnp.bitwise_xor(own, j) == quarter)
            def _(quarter=quarter, out=out):
                for k in range(outer):
                    part = xe[k][:, quarter * sub : (quarter + 1) * sub]
                    out[k * BLOCK : (k + 1) * BLOCK, rank:] = part


def pack(me, xe, sub, rank, outer):
    shape = jax.ShapeDtypeStruct((outer * BLOCK, rank + sub), BF)
    return pl.pallas_call(
        lambda *refs: pack_kernel(outer, sub, rank, *refs),
        out_shape=(shape,) * INNER,
        in_specs=[SM] + [VM] * outer,
        out_specs=(VM,) * INNER,
        compiler_params=params(24),
        cost_estimate=COST,
        name="pack_columns",
    )(me, *xe)


def down_kernel(per, blocks, rank, me_ref, ids_ref, *refs):
    out = refs[-1]
    first = pl.program_id(0) * per
    out[...] = jnp.zeros_like(out)

    for j, ref in enumerate(refs[:-1]):

        def each(k, carry, ref=ref, j=j):
            slot = ids_ref[jnp.bitwise_xor(me_ref[0], k * INNER + j)] - first

            @pl.when(jnp.logical_and(slot >= 0, slot < per))
            def _():
                rows = pl.ds(pl.multiple_of(k * BLOCK, BLOCK), BLOCK)
                out[slot] += dot(ref[rows, rank:], ref[rows, :rank], 0, 0)

            return carry

        lax.fori_loop(0, blocks, each, 0)


def down_grad(me, ids, packed, adapters, rank):
    shape = packed[0].shape
    sub = shape[1] - rank
    blocks = shape[0] // BLOCK
    per = 4
    whole = pl.BlockSpec(shape, lambda i, *_: (0, 0))
    return pl.pallas_call(
        lambda *refs: down_kernel(per, blocks, rank, *refs),
        grid_spec=pltpu.PrefetchScalarGridSpec(
            num_scalar_prefetch=2,
            grid=(adapters // per,),
            in_specs=[whole] * len(packed),
            out_specs=pl.BlockSpec((per, sub, rank), lambda i, *_: (i, 0, 0)),
        ),
        out_shape=jax.ShapeDtypeStruct((adapters, sub, rank), F32),
        compiler_params=params(32),
        cost_estimate=COST,
        name="down_gradient",
    )(me, ids, *packed)


def up_kernel(per, blocks, ids_ref, got, out):
    first = pl.program_id(0) * per
    out[...] = jnp.zeros_like(out)

    def each(i, carry):
        slot = ids_ref[i] - first

        @pl.when(jnp.logical_and(slot >= 0, slot < per))
        def _():
            out[slot] += got[i].astype(F32)

        return carry

    lax.fori_loop(0, blocks, each, 0)


def up_grad(ids, got, adapters):
    blocks, part, kv = got.shape
    per = 16
    return pl.pallas_call(
        lambda *refs: up_kernel(per, blocks, *refs),
        grid_spec=pltpu.PrefetchScalarGridSpec(
            num_scalar_prefetch=1,
            grid=(adapters // per,),
            in_specs=[pl.BlockSpec(got.shape, lambda i, *_: (0, 0, 0))],
            out_specs=pl.BlockSpec((per, part, kv), lambda i, *_: (i, 0, 0)),
        ),
        out_shape=jax.ShapeDtypeStruct((adapters, part, kv), F32),
        compiler_params=params(24),
        cost_estimate=COST,
        name="up_gradient",
    )(ids, got)


def join_kernel(outer, dz, me_ref, held_t, held_f, extra, *refs):
    got, parts, (proj, grad) = refs[: outer - 1], refs[outer - 1 : -2], refs[-2:]
    plane = lax.div(me_ref[0], INNER)
    for k in range(outer):
        at = pl.multiple_of(jnp.bitwise_xor(plane, k) * dz, dz)
        grad[:, pl.ds(at, dz)] = held_t[...] if k == 0 else got[k - 1][:, :dz]
    total = held_f[...] + extra[...] + got[0][:, dz:].astype(F32)
    proj[...] = (total + sum(p[...].astype(F32) for p in parts)).astype(BF)


def join(me, held_t, held_f, extra, got, parts):
    rows, dz = held_t.shape
    outer = 1 + len(got)
    return pl.pallas_call(
        lambda *refs: join_kernel(outer, dz, *refs),
        out_shape=(
            jax.ShapeDtypeStruct(held_f.shape, BF),
            jax.ShapeDtypeStruct((rows, dz * outer), BF),
        ),
        in_specs=[SM] + [VM] * (2 + outer + len(parts)),
        out_specs=(VM, VM),
        compiler_params=params(24),
        cost_estimate=COST,
        name="join_columns",
    )(me, held_t, held_f, extra, *got, *parts)


def build(devices):
    outer = devices // INNER

    def swap(value, mask):
        return lax.ppermute(value, "fsdp", [(i, i ^ mask) for i in range(devices)])

    def on_device(tokens, grad_out, base_weight, shrink_factor, expand_factor,
                  rank_per_adapter, block_adapter, block_rows):
        adapters, sub, rank = shrink_factor.shape
        kv = base_weight.shape[1]
        me = lax.axis_index("fsdp").reshape(1).astype(jnp.int32)

        def after(value, earlier):
            return lax.optimization_barrier((value, earlier))[0]

        def to_planes(parts):
            got = {k: swap(parts[k], k * INNER) for k in range(1, outer)}
            return [parts[0]] + [got[k] for k in range(1, outer)]

        masked = mask_rows(block_rows, grad_out)
        grads, evens = [masked], [0]
        step = outer // 2
        while step > 1:
            stack = grads[0] if len(grads) == 1 else jnp.concatenate(grads, axis=0)
            grads.append(swap(stack, step * INNER))
            evens = evens + [k ^ step for k in evens]
            step //= 2

        up_send = jnp.take(expand_factor, after(block_adapter, masked), axis=0, mode="clip")
        up = lax.all_to_all(up_send, "fsdp", split_axis=0, concat_axis=0, tiled=True)
        up = up.reshape(rank, kv)

        s_send, s_keep = pick(me, after(block_adapter, up_send), shrink_factor, outer)
        s_x = swap(after(s_send, (up, grads)), 2)
        w_x = swap(after(base_weight, (up, grads, s_keep)), 2)
        s_c = swap(after(s_keep, s_x)[outer:], 1)
        s_xc = swap(s_x[outer:], 1)
        w_c = swap(after(base_weight, w_x), 1)
        w_xc = [swap(w_x[: sub // 2], 1), swap(w_x[sub // 2 :], 1)]
        wparts = (base_weight, w_c, w_x, *w_xc)
        sparts = (s_keep, s_x, s_c, s_xc)

        cuts = first_sends(
            me, block_adapter, rank_per_adapter, tokens, after(up, s_keep), grads, outer
        )
        xe = to_planes(cuts)

        low = shrink_parts(me, sparts, xe, outer)
        products = main_parts(
            me, wparts, sparts, after(xe, low), grads, evens, outer
        )
        sends, held_f = products[:outer], products[outer]
        even_f, odd_f = products[outer + 1 : -1], products[-1]
        odd_got = swap(odd_f, INNER)
        low = to_planes(low)
        extra, eg = shrunk_rows(
            me, block_adapter, rank_per_adapter, after(low, products), up, masked
        )
        eg_got = eg.reshape(devices, rank // devices, kv)
        eg_got = lax.all_to_all(eg_got, "fsdp", split_axis=0, concat_axis=0, tiled=True)

        packed = pack(me, after(xe, eg), sub, rank, outer)
        core = swap(packed[1], 1)
        far = after(packed[2:], core)
        packed = [packed[0], core] + [swap(p, 2 + j) for j, p in enumerate(far)]
        shrink_grad = down_grad(me, block_adapter, packed, adapters, rank)
        expand_grad = up_grad(after(block_adapter, shrink_grad), eg_got, adapters)
        parts = []
        for i, value in enumerate(even_f):
            value = value + odd_got[i * BLOCK : (i + 1) * BLOCK].astype(F32)
            parts.append(swap(value.astype(BF), 2 * (i + 1) * INNER))
        held_t, *got = to_planes(sends)
        projected, token_input_gradient = join(
            me, held_t, held_f, extra, after(got, expand_grad), parts
        )
        return (projected, token_input_gradient, shrink_grad, expand_grad)

    return on_device


def solution(mesh):
    placed = (
        P(("groups", "fsdp"), None),
        P(("groups", "fsdp"), None),
        P("fsdp", None),
        P("groups", "fsdp", None),
        P("groups", "fsdp", None),
        P("groups"),
        P("groups"),
        P(("groups", "fsdp")),
    )
    return jax.shard_map(
        build(mesh.shape["fsdp"]),
        mesh=mesh,
        in_specs=placed,
        out_specs=(
            P(("groups", "fsdp"), None),
            P(("groups", "fsdp"), None),
            P("groups", "fsdp", None),
            P("groups", "fsdp", None),
        ),
        check_vma=False,
    )
```

```python
import jax
import jax.numpy as jnp
from jax import lax
from jax.experimental import pallas as pl
from jax.experimental.pallas import tpu as pltpu
from jax.sharding import PartitionSpec as P

BLOCK = 128
ADAPTER_STRENGTH = 16.0
INNER = 4
MIB = 1 << 20
BF = jnp.bfloat16
F32 = jnp.float32

HBM = pl.BlockSpec(memory_space=pltpu.HBM)
VM = pl.BlockSpec(memory_space=pltpu.VMEM)
SM = pl.BlockSpec(memory_space=pltpu.SMEM)


def params(mib):
    return pltpu.CompilerParams(vmem_limit_bytes=mib * MIB)


COST = pl.CostEstimate(flops=1, bytes_accessed=1, transcendentals=0)


def dot(a, b, ca, cb):
    return lax.dot_general(a, b, (((ca,), (cb,)), ((), ())), preferred_element_type=F32)


def adapter_scale(rank):
    return ADAPTER_STRENGTH / jnp.sqrt(jnp.full((BLOCK, BLOCK), rank, jnp.int32).astype(F32))


def pick_kernel(outer, me_ref, ids_ref, factor, s_send, s_keep, sem):
    def start(i, carry):
        core = lax.div(i, outer)
        own = jnp.bitwise_xor(me_ref[0], lax.rem(i, outer) * INNER + core)
        pltpu.make_async_copy(factor.at[ids_ref[own]], s_keep.at[i], sem.at[0]).start()
        far = jnp.bitwise_xor(own, 2)
        pltpu.make_async_copy(factor.at[ids_ref[far]], s_send.at[i], sem.at[1]).start()
        return carry

    half = s_keep.shape[0]
    lax.fori_loop(0, half, start, 0)
    pltpu.make_async_copy(factor.at[pl.ds(0, half)], s_keep, sem.at[0]).wait()
    pltpu.make_async_copy(factor.at[pl.ds(0, half)], s_send, sem.at[1]).wait()


def pick(me, ids, factor, outer):
    picked = jax.ShapeDtypeStruct((2 * outer,) + factor.shape[1:], BF)
    return pl.pallas_call(
        lambda *refs: pick_kernel(outer, *refs),
        out_shape=(picked, picked),
        in_specs=[SM, SM, HBM],
        out_specs=(VM, VM),
        scratch_shapes=[pltpu.SemaphoreType.DMA((2,))],
        compiler_params=params(57),
        cost_estimate=COST,
        name="pick_factors",
    )(me, ids, factor)


def mask_kernel(rows_ref, grad, out):
    rows = lax.broadcasted_iota(jnp.int32, grad.shape, 0)
    out[...] = jnp.where(rows < rows_ref[0], grad[...].astype(F32), 0.0).astype(BF)


def mask_rows(block_rows, grad):
    return pl.pallas_call(
        mask_kernel,
        out_shape=jax.ShapeDtypeStruct(grad.shape, BF),
        in_specs=[SM, VM],
        out_specs=VM,
        compiler_params=params(8),
        cost_estimate=COST,
        name="mask_rows",
    )(block_rows, grad)


def first_kernel(outer, me_ref, ids_ref, ranks_ref, tokens, up_ref, *refs):
    grads, outs = refs[:-outer], refs[-outer:]
    rank = ranks_ref[ids_ref[me_ref[0]]]
    plane = lax.div(me_ref[0], INNER)
    dz = tokens.shape[1] // outer
    rank_cap, kv = up_ref.shape
    back = dot(grads[0][...], up_ref[...], 1, 1) * adapter_scale(rank)
    cols = lax.broadcasted_iota(jnp.int32, back.shape, 1)
    back = jnp.where(cols < rank, back, 0.0).astype(BF)
    for k, out in enumerate(outs):
        at = pl.multiple_of(jnp.bitwise_xor(plane, k) * dz, dz)
        out[:, :dz] = tokens[:, pl.ds(at, dz)]
        out[:, dz : dz + rank_cap] = back
    at = dz + rank_cap
    for g in grads:
        for row in range(0, g.shape[0], BLOCK):
            outs[1][:, at : at + kv] = g[row : row + BLOCK, :]
            at += kv


def first_sends(me, ids, ranks, tokens, up, grads, outer):
    rows, width = tokens.shape
    rank_cap, kv = up.shape
    wide = width // outer + rank_cap
    more = outer // 2 * kv
    return pl.pallas_call(
        lambda *refs: first_kernel(outer, *refs),
        out_shape=tuple(
            jax.ShapeDtypeStruct((rows, wide + (more if k == 1 else 0)), BF)
            for k in range(outer)
        ),
        in_specs=[SM] * 3 + [VM] * (2 + len(grads)),
        out_specs=(VM,) * outer,
        compiler_params=params(32),
        cost_estimate=COST,
        name="first_sends",
    )(me, ids, ranks, tokens, up, *grads)


def plane_parts(me, w, s, scratch, outer, sub):
    own = lax.rem(me, INNER)
    parts = []
    for j, (ws, (ref, at)) in enumerate(zip(w, s)):
        first = pl.multiple_of(jnp.bitwise_xor(own, j) * sub, sub)
        row = 0
        for weight in ws:
            size = weight.shape[0]
            rows = slice(row, row + size)
            if scratch:
                wz, sz = scratch
                base = pl.multiple_of(first + row, size)
                wz[pl.ds(base, size), :] = weight[...]
                for k in range(outer):
                    sz[k, pl.ds(base, size), :] = ref[at + k, rows, :]
            else:
                base = pl.multiple_of(first + row, size)
                factors = [ref.at[at + k, rows] for k in range(outer)]
                parts.append((base, size, weight, factors))
            row += size
    if scratch:
        wz, sz = scratch
        parts = [(0, wz.shape[0], wz, [sz.at[k] for k in range(outer)])]
    return parts


def plane_scratch(outer, sub, kv, rank):
    if sub % 256 == 0:
        return []
    dz = sub * INNER
    return [pltpu.VMEM((dz, kv), BF), pltpu.VMEM((outer, dz, rank), BF)]


def main_kernel(evens, outer, sub, kv, me_ref, *refs):
    w = [[refs[0]], [refs[1]], [refs[2]], [refs[3], refs[4]]]
    s = [(refs[5], 0), (refs[7], 0), (refs[6], 0), (refs[8], 0)]
    rank = refs[5].shape[2]
    *ins, x, e = refs[9 : len(refs) - (0 if sub % 256 == 0 else 2)]
    scratch = refs[9 + len(ins) + 2 :]
    n_outs = 1 + outer + outer // 2
    ins, outs = ins[:-n_outs], ins[-n_outs:]
    held_t, *sends = outs[:outer]
    held_f = outs[outer]
    even_f = outs[outer + 1 : outer + outer // 2]
    odd_f = outs[outer + outer // 2 :]
    xe, grads = ins[:outer], ins[outer:]
    dz = sub * INNER
    for k in range(outer):
        x[k * BLOCK : (k + 1) * BLOCK, :] = xe[k][:, :dz]
    at = 0
    for g in grads:
        for row in range(0, g.shape[0], BLOCK):
            k = evens[at]
            e[k * BLOCK : (k + 1) * BLOCK, :] = g[row : row + BLOCK, :]
            first = dz + rank + at * kv
            k = k ^ 1
            e[k * BLOCK : (k + 1) * BLOCK, :] = xe[1][:, first : first + kv]
            at += 1
    parts = plane_parts(me_ref[0], w, s, scratch, outer, sub)
    for first, size, weight, factors in parts:
        base = dot(e[...], weight[...], 1, 1)
        for k in range(outer):
            extra = dot(xe[k][:, dz : dz + rank], factors[k][...], 1, 1)
            out = held_t if k == 0 else sends[k - 1]
            rows = slice(k * BLOCK, (k + 1) * BLOCK)
            out[:, pl.ds(first, size)] = (base[rows] + extra).astype(BF)
    step = 256
    for c in range(0, kv, step):
        part = sum(
            dot(x[:, pl.ds(first, size)], weight[:, c : c + step], 1, 0)
            for first, size, weight, _ in parts
        )
        for k in range(outer):
            value = part[k * BLOCK : (k + 1) * BLOCK]
            cols = slice(c, c + step)
            if k == 0:
                held_f[:, cols] = value
            elif k == 1:
                sends[0][:, dz + c : dz + c + step] = value.astype(BF)
            elif k % 2 == 0:
                even_f[k // 2 - 1][:, cols] = value
            else:
                row = (k // 2 - 1) * BLOCK
                odd_f[0][row : row + BLOCK, cols] = value.astype(BF)


def main_parts(me, wparts, sparts, xe, grads, evens, outer):
    sub, kv = wparts[0].shape
    rank = sparts[0].shape[-1]
    dz = sub * INNER
    half = outer // 2
    return pl.pallas_call(
        lambda *refs: main_kernel(evens, outer, sub, kv, *refs),
        out_shape=(
            jax.ShapeDtypeStruct((BLOCK, dz), BF),
            jax.ShapeDtypeStruct((BLOCK, dz + kv), BF),
        )
        + (jax.ShapeDtypeStruct((BLOCK, dz), BF),) * (outer - 2)
        + (jax.ShapeDtypeStruct((BLOCK, kv), F32),) * half
        + (jax.ShapeDtypeStruct(((half - 1) * BLOCK, kv), BF),),
        in_specs=[SM] + [VM] * (9 + outer + len(grads)),
        out_specs=(VM,) * (1 + outer + half),
        scratch_shapes=[
            pltpu.VMEM((outer * BLOCK, dz), BF),
            pltpu.VMEM((outer * BLOCK, kv), BF),
        ]
        + plane_scratch(outer, sub, kv, rank),
        compiler_params=params(48),
        cost_estimate=COST,
        name="plane_products",
    )(me, *wparts, *sparts, *xe, *grads)


def shrink_kernel(outer, sub, me_ref, *refs):
    s = [refs[0], refs[2], refs[1], refs[3]]
    xe = refs[4 : 4 + outer]
    outs = refs[4 + outer : 4 + 2 * outer]
    scratch = refs[4 + 2 * outer :]
    own = lax.rem(me_ref[0], INNER)
    for k in range(outer):
        total = None
        for j, ref in enumerate(s):
            first = pl.multiple_of(jnp.bitwise_xor(own, j) * sub, sub)
            if scratch:
                scratch[0][pl.ds(first, sub), :] = ref[k]
            else:
                term = dot(xe[k][:, pl.ds(first, sub)], ref[k], 1, 0)
                total = term if total is None else total + term
        if scratch:
            total = dot(xe[k][:, : sub * INNER], scratch[0][...], 1, 0)
        outs[k][...] = total


def shrink_parts(me, sparts, xe, outer):
    sub, rank = sparts[0].shape[1:]
    scratch = [] if sub % 128 == 0 else [pltpu.VMEM((sub * INNER, rank), BF)]
    return pl.pallas_call(
        lambda *refs: shrink_kernel(outer, sub, *refs),
        out_shape=tuple(jax.ShapeDtypeStruct((BLOCK, rank), F32) for _ in range(outer)),
        in_specs=[SM] + [VM] * (4 + outer),
        out_specs=(VM,) * outer,
        scratch_shapes=scratch,
        compiler_params=params(24),
        cost_estimate=COST,
        name="shrink_parts",
    )(me, *sparts, *xe)


def rows_kernel(outer, me_ref, ids_ref, ranks_ref, *refs):
    parts = refs[:outer]
    up, own, extra, eg = refs[outer:]
    rank = ranks_ref[ids_ref[me_ref[0]]]
    low = sum(p[...] for p in parts)
    cols = lax.broadcasted_iota(jnp.int32, low.shape, 1)
    shrink = jnp.where(cols < rank, low, 0.0).astype(BF)
    scale = adapter_scale(rank)[:, :1]
    extra[...] = dot(shrink, up[...], 1, 0) * scale
    eg[...] = (dot(shrink, own[...], 0, 0) * scale).astype(BF)


def shrunk_rows(me, ids, ranks, parts, up, own):
    rank_cap, kv = up.shape
    outer = len(parts)
    return pl.pallas_call(
        lambda *refs: rows_kernel(outer, *refs),
        out_shape=(
            jax.ShapeDtypeStruct((BLOCK, kv), F32),
            jax.ShapeDtypeStruct((rank_cap, kv), BF),
        ),
        in_specs=[SM, SM, SM] + [VM] * (outer + 2),
        out_specs=(VM, VM),
        compiler_params=params(24),
        cost_estimate=COST,
        name="shrunk_rows",
    )(me, ids, ranks, *parts, up, own)


def pack_kernel(outer, sub, rank, me_ref, *refs):
    xe, outs = refs[:outer], refs[outer:]
    own = lax.rem(me_ref[0], INNER)
    last = sub * INNER
    for j, out in enumerate(outs):
        for k in range(outer):
            out[k * BLOCK : (k + 1) * BLOCK, :rank] = xe[k][:, last : last + rank]
        for quarter in range(INNER):

            @pl.when(jnp.bitwise_xor(own, j) == quarter)
            def _(quarter=quarter, out=out):
                for k in range(outer):
                    part = xe[k][:, quarter * sub : (quarter + 1) * sub]
                    out[k * BLOCK : (k + 1) * BLOCK, rank:] = part


def pack(me, xe, sub, rank, outer):
    shape = jax.ShapeDtypeStruct((outer * BLOCK, rank + sub), BF)
    return pl.pallas_call(
        lambda *refs: pack_kernel(outer, sub, rank, *refs),
        out_shape=(shape,) * INNER,
        in_specs=[SM] + [VM] * outer,
        out_specs=(VM,) * INNER,
        compiler_params=params(24),
        cost_estimate=COST,
        name="pack_columns",
    )(me, *xe)


def down_kernel(per, blocks, rank, me_ref, ids_ref, *refs):
    out = refs[-1]
    first = pl.program_id(0) * per
    out[...] = jnp.zeros_like(out)

    for j, ref in enumerate(refs[:-1]):

        def each(k, carry, ref=ref, j=j):
            slot = ids_ref[jnp.bitwise_xor(me_ref[0], k * INNER + j)] - first

            @pl.when(jnp.logical_and(slot >= 0, slot < per))
            def _():
                rows = pl.ds(pl.multiple_of(k * BLOCK, BLOCK), BLOCK)
                out[slot] += dot(ref[rows, rank:], ref[rows, :rank], 0, 0)

            return carry

        lax.fori_loop(0, blocks, each, 0)


def down_grad(me, ids, packed, adapters, rank):
    shape = packed[0].shape
    sub = shape[1] - rank
    blocks = shape[0] // BLOCK
    per = 4
    whole = pl.BlockSpec(shape, lambda i, *_: (0, 0))
    return pl.pallas_call(
        lambda *refs: down_kernel(per, blocks, rank, *refs),
        grid_spec=pltpu.PrefetchScalarGridSpec(
            num_scalar_prefetch=2,
            grid=(adapters // per,),
            in_specs=[whole] * len(packed),
            out_specs=pl.BlockSpec((per, sub, rank), lambda i, *_: (i, 0, 0)),
        ),
        out_shape=jax.ShapeDtypeStruct((adapters, sub, rank), F32),
        compiler_params=params(32),
        cost_estimate=COST,
        name="down_gradient",
    )(me, ids, *packed)


def up_kernel(per, blocks, ids_ref, got, out):
    first = pl.program_id(0) * per
    out[...] = jnp.zeros_like(out)

    def each(i, carry):
        slot = ids_ref[i] - first

        @pl.when(jnp.logical_and(slot >= 0, slot < per))
        def _():
            out[slot] += got[i].astype(F32)

        return carry

    lax.fori_loop(0, blocks, each, 0)


def up_grad(ids, got, adapters):
    blocks, part, kv = got.shape
    per = 16
    return pl.pallas_call(
        lambda *refs: up_kernel(per, blocks, *refs),
        grid_spec=pltpu.PrefetchScalarGridSpec(
            num_scalar_prefetch=1,
            grid=(adapters // per,),
            in_specs=[pl.BlockSpec(got.shape, lambda i, *_: (0, 0, 0))],
            out_specs=pl.BlockSpec((per, part, kv), lambda i, *_: (i, 0, 0)),
        ),
        out_shape=jax.ShapeDtypeStruct((adapters, part, kv), F32),
        compiler_params=params(24),
        cost_estimate=COST,
        name="up_gradient",
    )(ids, got)


def join_kernel(outer, dz, me_ref, held_t, held_f, extra, *refs):
    got, parts, (proj, grad) = refs[: outer - 1], refs[outer - 1 : -2], refs[-2:]
    plane = lax.div(me_ref[0], INNER)
    for k in range(outer):
        at = pl.multiple_of(jnp.bitwise_xor(plane, k) * dz, dz)
        grad[:, pl.ds(at, dz)] = held_t[...] if k == 0 else got[k - 1][:, :dz]
    total = held_f[...] + extra[...] + got[0][:, dz:].astype(F32)
    proj[...] = (total + sum(p[...].astype(F32) for p in parts)).astype(BF)


def join(me, held_t, held_f, extra, got, parts):
    rows, dz = held_t.shape
    outer = 1 + len(got)
    return pl.pallas_call(
        lambda *refs: join_kernel(outer, dz, *refs),
        out_shape=(
            jax.ShapeDtypeStruct(held_f.shape, BF),
            jax.ShapeDtypeStruct((rows, dz * outer), BF),
        ),
        in_specs=[SM] + [VM] * (2 + outer + len(parts)),
        out_specs=(VM, VM),
        compiler_params=params(24),
        cost_estimate=COST,
        name="join_columns",
    )(me, held_t, held_f, extra, *got, *parts)


def build(devices):
    outer = devices // INNER

    def swap(value, mask):
        return lax.ppermute(value, "fsdp", [(i, i ^ mask) for i in range(devices)])

    def on_device(tokens, grad_out, base_weight, shrink_factor, expand_factor,
                  rank_per_adapter, block_adapter, block_rows):
        adapters, sub, rank = shrink_factor.shape
        kv = base_weight.shape[1]
        me = lax.axis_index("fsdp").reshape(1).astype(jnp.int32)

        def after(value, earlier):
            return lax.optimization_barrier((value, earlier))[0]

        def to_planes(parts):
            got = {k: swap(parts[k], k * INNER) for k in range(1, outer)}
            return [parts[0]] + [got[k] for k in range(1, outer)]

        masked = mask_rows(block_rows, grad_out)
        grads, evens = [masked], [0]
        step = outer // 2
        while step > 1:
            stack = grads[0] if len(grads) == 1 else jnp.concatenate(grads, axis=0)
            grads.append(swap(stack, step * INNER))
            evens = evens + [k ^ step for k in evens]
            step //= 2

        up_send = jnp.take(expand_factor, block_adapter, axis=0, mode="clip")
        up = lax.all_to_all(up_send, "fsdp", split_axis=0, concat_axis=0, tiled=True)
        up = up.reshape(rank, kv)

        s_send, s_keep = pick(me, after(block_adapter, up_send), shrink_factor, outer)
        s_x = swap(after(s_send, (up, grads)), 2)
        w_x = swap(after(base_weight, (up, grads, s_keep)), 2)
        s_c = swap(after(s_keep, s_x)[outer:], 1)
        s_xc = swap(s_x[outer:], 1)
        w_c = swap(after(base_weight, w_x), 1)
        w_xc = [swap(w_x[: sub // 2], 1), swap(w_x[sub // 2 :], 1)]
        wparts = (base_weight, w_c, w_x, *w_xc)
        sparts = (s_keep, s_x, s_c, s_xc)

        cuts = first_sends(
            me, block_adapter, rank_per_adapter, tokens, after(up, s_keep), grads, outer
        )
        xe = to_planes(cuts)

        low = shrink_parts(me, sparts, xe, outer)
        products = main_parts(
            me, wparts, sparts, after(xe, low), grads, evens, outer
        )
        sends, held_f = products[:outer], products[outer]
        even_f, odd_f = products[outer + 1 : -1], products[-1]
        odd_got = swap(odd_f, INNER)
        low = to_planes(low)
        extra, eg = shrunk_rows(
            me, block_adapter, rank_per_adapter, after(low, products), up, masked
        )
        eg_got = eg.reshape(devices, rank // devices, kv)
        eg_got = lax.all_to_all(eg_got, "fsdp", split_axis=0, concat_axis=0, tiled=True)

        packed = pack(me, after(xe, eg), sub, rank, outer)
        core = swap(packed[1], 1)
        far = after(packed[2:], core)
        packed = [packed[0], core] + [swap(p, 2 + j) for j, p in enumerate(far)]
        shrink_grad = down_grad(me, block_adapter, packed, adapters, rank)
        expand_grad = up_grad(after(block_adapter, shrink_grad), eg_got, adapters)
        parts = []
        for i, value in enumerate(even_f):
            value = value + odd_got[i * BLOCK : (i + 1) * BLOCK].astype(F32)
            parts.append(swap(value.astype(BF), 2 * (i + 1) * INNER))
        held_t, *got = to_planes(sends)
        projected, token_input_gradient = join(
            me, held_t, held_f, extra, after(got, expand_grad), parts
        )
        return (projected, token_input_gradient, shrink_grad, expand_grad)

    return on_device


def solution(mesh):
    placed = (
        P(("groups", "fsdp"), None),
        P(("groups", "fsdp"), None),
        P("fsdp", None),
        P("groups", "fsdp", None),
        P("groups", "fsdp", None),
        P("groups"),
        P("groups"),
        P(("groups", "fsdp")),
    )
    return jax.shard_map(
        build(mesh.shape["fsdp"]),
        mesh=mesh,
        in_specs=placed,
        out_specs=(
            P(("groups", "fsdp"), None),
            P(("groups", "fsdp"), None),
            P("groups", "fsdp", None),
            P("groups", "fsdp", None),
        ),
        check_vma=False,
    )
```
